32 devices in a mesh: alpha: 8 (over z, core), beta: 4 (over y, x).
Axes of the slice: x: 2, y: 2, z: 4, core: 2. Of those that a mesh axis runs over, the one named last changes fastest.
Arguments:
- coefficients: bfloat16 [4096, 4096], P('alpha', 'beta'), may hold values from -6 to 6
- diagonal: float32 [4096, 4096], P('alpha', 'beta'), may hold values from 0.5 to 2
- alpha_blocks: bfloat16 [32, 14, 128, 128], P('alpha'), may hold values from -0.125 to 0.125
- alpha_lists: int32 [32, 14], replicated, may hold values from 0 to 31, as said below
- beta_blocks: bfloat16 [32, 14, 128, 128], P('beta'), may hold values from -0.125 to 0.125
- beta_lists: int32 [32, 14], replicated, may hold values from 0 to 31, as said below
Outputs:
- sigma_out: bfloat16 [4096, 4096], P('alpha', 'beta')
The draws below stay inside these ranges and needn't reach their ends.
Inputs may be any that keep to these rules, and one draw needn't show every extreme that they name: `alpha_lists`: each row names 14 different blocks. For every alpha device, the rows of its 4 block rows name at most 2 different blocks owned by any one alpha device (blocks j * 4 to (j + 1) * 4 - 1 belong to device j), and exactly 2 from some owner. `beta_lists`: each row names 14 different blocks. For every beta device, the rows of its 8 block rows name at most 4 different blocks owned by any one beta device (blocks j * 8 to (j + 1) * 8 - 1 belong to device j), and exactly 4 from some owner.
All inputs are finite; a program needn't handle non-finite values.
Results may differ from the reference program's by a relative error of at most 0.001.
Values may be sent and summed in bfloat16 or wider, within the bound.
No kernel may reach another device: no remote copies, remote signals or barrier semaphores. Data moves between devices by JAX's collectives and lax.ppermute only.
A program may use at most 128 MiB of HBM per device.

```python
import jax
import jax.numpy as jnp
from jax import lax

BLK = 128
SLOTS = 14
RA = 4
RB = 8
CAP_A = 2
CAP_B = 4
NBR_A = 32
NBR_B = 32
NA = 4096
NB = 4096


def draw_lists(key, owners, per_owner, limit):
    key_pick, key_rows, key_force = jax.random.split(key, 3)
    order_scores = jax.random.randint(key_pick, (owners, owners, per_owner), 0, 2 ** 20) * per_owner + jnp.arange(per_owner, dtype=jnp.int32)
    order = jnp.argsort(order_scores, axis=-1)[..., :limit].astype(jnp.int32)
    candidates = (jnp.arange(owners, dtype=jnp.int32)[None, :, None] * per_owner + order).reshape(owners, owners * limit)
    total = owners * limit
    forced = jax.random.randint(key_force, (owners,), 0, owners)
    position = jnp.arange(total, dtype=jnp.int32)
    row_scores = jax.random.randint(key_rows, (owners, per_owner, total), 0, 2 ** 20) * total + position
    force_mask = (jnp.arange(per_owner)[None, :, None] == 0) & ((position // limit)[None, None, :] == forced[:, None, None])
    row_scores = jnp.where(force_mask, position - total, row_scores)
    picks = jnp.argsort(row_scores, axis=-1)[..., :SLOTS]
    spread = jnp.broadcast_to(candidates[:, None, :], (owners, per_owner, total))
    chosen = jnp.take_along_axis(spread, picks, axis=-1)
    return chosen.reshape(owners * per_owner, SLOTS).astype(jnp.int32)


def draw_alpha_lists(key, part):
    return draw_lists(jax.random.fold_in(key, 11), NBR_A // RA, RA, CAP_A)


def draw_beta_lists(key, part):
    return draw_lists(jax.random.fold_in(key, 23), NBR_B // RB, RB, CAP_B)


def block_scale(key, dims, pieces, smallest, largest):
    factor_of = 1.0
    for dim, blocks in pieces:
        draws = jax.random.uniform(jax.random.fold_in(jax.random.fold_in(key, 6), dim), (blocks,), jnp.float32, smallest / len(pieces), largest / len(pieces))
        factor_of = factor_of * jnp.repeat(jnp.exp(draws), dims[dim] // blocks).reshape((-1,) + (1,) * (len(dims) - 1 - dim))
    return factor_of


def scatter_about(own_key, extent, width, most, cuts=(), held_as=jnp.bfloat16):
    gain = block_scale(own_key, extent, cuts, -0.22, 0.18) if cuts else 1.0
    array = jax.random.normal(own_key, extent, jnp.float32) * width * gain
    return jnp.minimum(jnp.maximum(array, -most), most).astype(held_as)


def setup_inputs(seed: int = 0) -> dict:
    keys = jax.random.split(jax.random.key(seed), 7)
    coefficients = scatter_about(keys[0], (NA, NB), 1.0, 6.0, ((0, 8), (1, 4)))
    diagonal = jnp.clip(0.5 + 1.5 * jax.random.uniform(keys[1], (NA, NB), jnp.float32) ** block_scale(keys[1], (NA, NB), ((0, 8), (1, 4)), -0.2, 0.2), 0.5, 2.0)
    alpha_blocks = scatter_about(keys[2], (NBR_A, SLOTS, BLK, BLK), (SLOTS * BLK) ** -0.5, 0.125, ((0, 8),))
    alpha_lists = draw_alpha_lists(jax.random.fold_in(keys[6], 71), 0)
    beta_blocks = scatter_about(keys[4], (NBR_B, SLOTS, BLK, BLK), (SLOTS * BLK) ** -0.5, 0.125, ((0, 4),))
    beta_lists = draw_beta_lists(jax.random.fold_in(keys[6], 71), 0)
    return dict(coefficients=coefficients, diagonal=diagonal, alpha_blocks=alpha_blocks, alpha_lists=alpha_lists, beta_blocks=beta_blocks, beta_lists=beta_lists)


def alpha_part(coefficients, alpha_blocks, alpha_lists):
    stacked = coefficients.astype(jnp.float32).reshape(NBR_A, BLK, NB)

    def one_row(row_args):
        blocks_here, list_ids = row_args
        fetched = jnp.take(stacked, list_ids, axis=0)
        return jnp.einsum("kab,kbn->an", blocks_here.astype(jnp.float32), fetched)

    rows_out = lax.map(one_row, (alpha_blocks, alpha_lists))
    return rows_out.reshape(NA, NB)


def beta_part(coefficients, beta_blocks, beta_lists):
    stacked = coefficients.astype(jnp.float32).reshape(NA, NBR_B, BLK)

    def one_col(col_args):
        blocks_here, list_ids = col_args
        fetched = jnp.take(stacked, list_ids, axis=1)
        return jnp.einsum("mkb,kab->ma", fetched, blocks_here.astype(jnp.float32))

    cols_out = lax.map(one_col, (beta_blocks, beta_lists))
    return jnp.transpose(cols_out, (1, 0, 2)).reshape(NA, NB)


def reference(coefficients, diagonal, alpha_blocks, alpha_lists, beta_blocks, beta_lists):
    alpha_term = alpha_part(coefficients, alpha_blocks, alpha_lists)
    beta_term = beta_part(coefficients, beta_blocks, beta_lists)
    total = alpha_term + beta_term + diagonal * coefficients.astype(jnp.float32)
    return total.astype(jnp.bfloat16)
```

```python
import functools

import jax
import jax.numpy as jnp
import numpy as np
from jax import lax
from jax.experimental import pallas as pl
from jax.experimental.pallas import tpu as pltpu
from jax.sharding import PartitionSpec as P

CAP_B = 4
CORES = 2
STEP = 1
VMEM_LIMIT = 40 * 1024 * 1024


def beta_tables(beta_lists, me, owners, per_owner):
    number = owners * per_owner
    ids = jnp.arange(number, dtype=jnp.int32)
    flat = beta_lists.reshape(owners, -1)
    needed = jnp.any(flat[:, :, None] == ids, axis=1)
    same = (ids[:, None] // per_owner == ids[None, :] // per_owner) & (ids[:, None] < ids[None, :])
    rank = jnp.sum((needed[:, :, None] & same).astype(jnp.int32), axis=1)
    caps = jnp.arange(CAP_B, dtype=jnp.int32)
    match = needed[:, :, None] & (rank[:, :, None] == caps)
    match = match.reshape(owners, owners, per_owner, CAP_B)
    local = jnp.arange(per_owner, dtype=jnp.int32)[:, None]
    chosen = jnp.max(jnp.where(match, local, -1), axis=2)
    steps = np.arange(1, owners)
    pack = lax.dynamic_index_in_dim(chosen, me, 1, keepdims=False)
    pack = jnp.take(pack, partner(me, steps, owners), axis=0)
    got = lax.dynamic_index_in_dim(chosen, me, 0, keepdims=False)
    got = jnp.where(got >= 0, got + jnp.arange(owners, dtype=jnp.int32)[:, None] * per_owner, -1)
    got = jnp.take(got, partner_back(me, steps, owners), axis=0).reshape(-1)
    got = jnp.concatenate([me * per_owner + jnp.arange(per_owner, dtype=jnp.int32), got])
    return jnp.maximum(pack, 0).reshape(-1), got


def partner(me, step, owners):
    if owners & (owners - 1) == 0:
        return me ^ step
    return (me + step) % owners


def partner_back(me, step, owners):
    if owners & (owners - 1) == 0:
        return me ^ step
    return (me + owners - step) % owners


def slot_table(lists, position_ids):
    slots = jnp.arange(lists.shape[1], dtype=jnp.int32)[None, :, None]
    hit = lists[:, :, None] == position_ids[None, None, :]
    return jnp.max(jnp.where(hit, slots, -1), axis=1)


def pack_beta_body(block, pack_ref, c_ref, *outs):
    for s, out in enumerate(outs):
        for c in range(CAP_B):
            j = pack_ref[s * CAP_B + c]
            column = pl.ds(pl.multiple_of(j * block, block), block)
            out[:, c * block : (c + 1) * block] = c_ref[:, column]


def pack_beta(pack, coefficients, parts, block):
    height = coefficients.shape[0]
    shape = jax.ShapeDtypeStruct((height, CAP_B * block), coefficients.dtype)
    return pl.pallas_call(
        functools.partial(pack_beta_body, block),
        grid_spec=pltpu.PrefetchScalarGridSpec(
            num_scalar_prefetch=1,
            grid=(),
            in_specs=[pl.BlockSpec(memory_space=pltpu.VMEM)],
            out_specs=[pl.BlockSpec(memory_space=pltpu.VMEM)] * parts,
        ),
        out_shape=[shape] * parts,
        compiler_params=pltpu.CompilerParams(vmem_limit_bytes=VMEM_LIMIT),
        name="pack_beta",
    )(pack, coefficients)


def fill(weights, table_ref, h_ref, rows, positions, block, first=0):
    for i in range(first, first + rows):
        for q in range(positions):
            k = table_ref[i * positions + q]
            tile = h_ref[i - first, jnp.maximum(k, 0)]
            weights[i * block : (i + 1) * block, q * block : (q + 1) * block] = jnp.where(
                k >= 0, tile, jnp.zeros_like(tile)
            )


def beta_body(rows, positions, block, table_ref, h_ref, d_ref, c_ref, *rest):
    arrived, out_ref, weights = rest[:-2], rest[-2], rest[-1]
    fill(weights, table_ref, h_ref, rows, positions, block)
    own = c_ref[...]
    x = jnp.concatenate([own] + [a[...] for a in arrived], axis=1)
    total = lax.dot_general(
        x, weights[...], (((1,), (1,)), ((), ())), preferred_element_type=jnp.float32
    )
    out_ref[...] = total + d_ref[...] * own.astype(jnp.float32)


def beta_product(table, beta_blocks, coefficients, diagonal, arrived):
    rows, block = beta_blocks.shape[0], beta_blocks.shape[2]
    positions = table.shape[1]
    return pl.pallas_call(
        functools.partial(beta_body, rows, positions, block),
        grid_spec=pltpu.PrefetchScalarGridSpec(
            num_scalar_prefetch=1,
            grid=(),
            in_specs=[pl.BlockSpec(memory_space=pltpu.VMEM)] * (3 + len(arrived)),
            out_specs=pl.BlockSpec(memory_space=pltpu.VMEM),
            scratch_shapes=[pltpu.VMEM((rows * block, positions * block), jnp.bfloat16)],
        ),
        out_shape=jax.ShapeDtypeStruct(diagonal.shape, jnp.float32),
        compiler_params=pltpu.CompilerParams(vmem_limit_bytes=VMEM_LIMIT),
        name="beta_product",
    )(table.reshape(-1), beta_blocks, diagonal, coefficients, *arrived)


def alpha_body(rows, positions, block, table_ref, h_refs, add_refs, piece_refs, out_refs, weights):
    for n, h_ref in enumerate(h_refs):
        fill(weights, table_ref, h_ref, rows, positions, block, n * rows)
    x = jnp.concatenate([p[...] for p in piece_refs], axis=0)
    height = rows * block
    for n, out_ref in enumerate(out_refs):
        total = jnp.dot(weights[n * height : (n + 1) * height], x, preferred_element_type=jnp.float32)
        if add_refs:
            total = total + add_refs[n][...]
        out_ref[...] = total.astype(out_ref.dtype)


def alpha_product(table, blocks, adds, pieces, dtype):
    rows, block = blocks[0].shape[0], blocks[0].shape[2]
    positions = table.shape[1]
    height, width = rows * block, pieces[0].shape[1]

    def body(table_ref, *rest):
        h_refs, rest = rest[: len(blocks)], rest[len(blocks) :]
        add_refs, rest = rest[: len(adds)], rest[len(adds) :]
        piece_refs, rest = rest[: len(pieces)], rest[len(pieces) :]
        alpha_body(rows, positions, block, table_ref, h_refs, add_refs, piece_refs, rest[:-1], rest[-1])

    return pl.pallas_call(
        body,
        grid_spec=pltpu.PrefetchScalarGridSpec(
            num_scalar_prefetch=1,
            grid=(),
            in_specs=[pl.BlockSpec(memory_space=pltpu.VMEM)] * (len(blocks) + len(adds) + len(pieces)),
            out_specs=[pl.BlockSpec(memory_space=pltpu.VMEM)] * len(blocks),
            scratch_shapes=[pltpu.VMEM((len(blocks) * height, positions * block), jnp.bfloat16)],
        ),
        out_shape=[jax.ShapeDtypeStruct((height, width), dtype)] * len(blocks),
        compiler_params=pltpu.CompilerParams(vmem_limit_bytes=VMEM_LIMIT),
        name="alpha_product",
    )(table.reshape(-1), *blocks, *adds, *pieces)


def send(x, edges):
    return lax.ppermute(x, "alpha", [(s * CORES + c, t * CORES + c) for s, t in edges for c in range(CORES)])


def swap(x, chips):
    return lax.ppermute(x, "alpha", [(p * CORES + c, p * CORES + 1 - c) for p in chips for c in range(CORES)])


def gate(*values):
    return lax.optimization_barrier(values)


def block_ids(places, rows):
    ids = np.full((len(places), CORES, len(places[0])), -1, np.int32)
    for p, line in enumerate(places):
        for g, place in enumerate(line):
            if place is not None:
                for c in range(CORES):
                    ids[p, c, g] = (place[0] * CORES + c) * rows + place[1]
    return ids


def per_device(coefficients, diagonal, alpha_blocks, alpha_lists, beta_blocks, beta_lists):
    block = alpha_blocks.shape[2]
    rows_a, rows_b = alpha_blocks.shape[0], beta_blocks.shape[0]
    chips = lax.axis_size("alpha") // CORES
    owners_b = lax.axis_size("beta")
    index_a, index_b = lax.axis_index("alpha"), lax.axis_index("beta")
    core = lax.rem(index_a, CORES)
    height = rows_a * block
    span = STEP * block
    cuts = rows_a // STEP

    pack, beta_ids = beta_tables(beta_lists, index_b, owners_b, rows_b)
    mine_b = lax.dynamic_slice_in_dim(beta_lists, index_b * rows_b, rows_b, 0)

    def place(chip, first, count):
        return [(chip, first + g) if 0 <= chip < chips else None for g in range(count)]

    def table_of(places, lists, swapped):
        ids = [block_ids(p, rows_a) for p in places]
        if swapped:
            ids = ids + [i[:, ::-1] for i in ids]
        ids = jnp.asarray(np.concatenate(ids, axis=2).reshape(chips * CORES, -1))
        return slot_table(lists, lax.dynamic_index_in_dim(ids, index_a, 0, keepdims=False))

    mine_a = lax.dynamic_slice_in_dim(alpha_lists, index_a * rows_a, rows_a, 0)
    theirs_a = lax.dynamic_slice_in_dim(alpha_lists, (index_a + 1 - 2 * core) * rows_a, rows_a, 0)
    both = jnp.concatenate([mine_a, theirs_a], axis=0)
    table_b = slot_table(mine_b, beta_ids)

    def beta_all(arrived):
        return beta_product(table_b, beta_blocks, coefficients, diagonal, arrived)

    def exchange(packed):
        steps = range(1, owners_b)
        return [
            lax.ppermute(packed[s - 1], "beta", [(d, partner(d, s, owners_b)) for d in range(owners_b)]) for s in steps
        ]

    def product(table, pieces, adds):
        return alpha_product(table, [alpha_blocks, other_blocks], adds, pieces, jnp.float32)

    def last_product(table, pieces, acc):
        return alpha_product(table, [alpha_blocks], [acc], pieces, jnp.bfloat16)[0]

    everyone = range(chips)
    own = [place(p, 0, rows_a) for p in everyone]
    if chips == 4:
        far, near = [(0, 2), (1, 3), (2, 0), (3, 1)], [(0, 1), (1, 0), (2, 3), (3, 2)]
        far_from, near_from, both_from = [2, 3, 0, 1], [1, 0, 3, 2], [3, 2, 1, 0]

        def of(chip_of):
            return [place(chip_of[p], 0, rows_a) for p in everyone]

        table_here = table_of([own, of(near_from), of(far_from)], mine_a, True)
        table_both = table_of([of(both_from)], mine_a, True)

        near_own, far_own = send(coefficients, near), send(coefficients, far)
        arrived = exchange(pack_beta(pack, coefficients, owners_b - 1, block))
        near_own, far_own, here, table_here, table_both, table_b, *arrived = gate(
            near_own, far_own, coefficients, table_here, table_both, table_b, *arrived
        )

        near_far = send(far_own, near)
        pieces = [here, near_own, far_own]
        pieces += [swap(x, everyone) for x in pieces]
        *pieces, here = gate(*pieces, here)
        acc = beta_product(table_b, beta_blocks, here, diagonal, arrived)
        (acc,) = alpha_product(table_here, [alpha_blocks], [acc], pieces, jnp.float32)
        near_far, acc = gate(near_far, acc)
        return last_product(table_both, [near_far, swap(near_far, everyone)], acc)

    other_blocks = swap(alpha_blocks, everyone)
    arrived = exchange(pack_beta(pack, coefficients, owners_b - 1, block))
    pieces, places = [coefficients], [own]
    left, right = [], []
    for u in range((chips - 1) * cuts):
        kind, v = u // cuts, u % cuts
        mine = coefficients[v * span : (v + 1) * span]
        left.append(send(mine if u < cuts else left[u - cuts], [(p, p - 1) for p in range(1, chips) if kind < chips - p]))
        right.append(send(mine if u < cuts else right[u - cuts], [(p, p + 1) for p in range(chips - 1) if kind < p + 1]))
        pieces += [left[u], right[u]]
        places += [
            [place(p + 1 + kind, v * STEP, STEP) for p in everyone],
            [place(p - 1 - kind, v * STEP, STEP) for p in everyone],
        ]
    sums = []
    for k in range(0, len(pieces) - 2, 4):
        upto = min(k + 4, len(pieces) - 2)
        sums = product(table_of(places[k:upto], both, False), pieces[k:upto], sums)
    acc = beta_all(arrived) + sums[0] + swap(sums[1], everyone)
    ends = pieces[-2:]
    return last_product(table_of(places[-2:], mine_a, True), ends + [swap(x, everyone) for x in ends], acc)


def solution(mesh):
    in_specs = (
        P("alpha", "beta"),
        P("alpha", "beta"),
        P("alpha", None, None, None),
        P(),
        P("beta", None, None, None),
        P(),
    )
    out_specs = P("alpha", "beta")
    return jax.shard_map(
        per_device, mesh=mesh, in_specs=in_specs, out_specs=out_specs, check_vma=False
    )
```

```python
import functools

import jax
import jax.numpy as jnp
import numpy as np
from jax import lax
from jax.experimental import pallas as pl
from jax.experimental.pallas import tpu as pltpu
from jax.sharding import PartitionSpec as P

CAP_B = 4
CORES = 2
VMEM_LIMIT = 40 * 1024 * 1024


def beta_tables(beta_lists, me, owners, per_owner):
    number = owners * per_owner
    ids = jnp.arange(number, dtype=jnp.int32)
    flat = beta_lists.reshape(owners, -1)
    needed = jnp.any(flat[:, :, None] == ids, axis=1)
    same = (ids[:, None] // per_owner == ids[None, :] // per_owner) & (ids[:, None] < ids[None, :])
    rank = jnp.sum((needed[:, :, None] & same).astype(jnp.int32), axis=1)
    caps = jnp.arange(CAP_B, dtype=jnp.int32)
    match = needed[:, :, None] & (rank[:, :, None] == caps)
    match = match.reshape(owners, owners, per_owner, CAP_B)
    local = jnp.arange(per_owner, dtype=jnp.int32)[:, None]
    chosen = jnp.max(jnp.where(match, local, -1), axis=2)
    steps = np.arange(1, owners)
    pack = lax.dynamic_index_in_dim(chosen, me, 1, keepdims=False)
    pack = jnp.take(pack, partner(me, steps, owners), axis=0)
    got = lax.dynamic_index_in_dim(chosen, me, 0, keepdims=False)
    got = jnp.where(got >= 0, got + jnp.arange(owners, dtype=jnp.int32)[:, None] * per_owner, -1)
    got = jnp.take(got, partner_back(me, steps, owners), axis=0).reshape(-1)
    got = jnp.concatenate([me * per_owner + jnp.arange(per_owner, dtype=jnp.int32), got])
    return jnp.maximum(pack, 0).reshape(-1), got


def partner(me, step, owners):
    if owners & (owners - 1) == 0:
        return me ^ step
    return (me + step) % owners


def partner_back(me, step, owners):
    if owners & (owners - 1) == 0:
        return me ^ step
    return (me + owners - step) % owners


def slot_table(lists, position_ids):
    slots = jnp.arange(lists.shape[1], dtype=jnp.int32)[None, :, None]
    hit = lists[:, :, None] == position_ids[None, None, :]
    return jnp.max(jnp.where(hit, slots, -1), axis=1)


def pack_beta_body(block, pack_ref, c_ref, *outs):
    for s, out in enumerate(outs):
        for c in range(CAP_B):
            j = pack_ref[s * CAP_B + c]
            column = pl.ds(pl.multiple_of(j * block, block), block)
            out[:, c * block : (c + 1) * block] = c_ref[:, column]


def pack_beta(pack, coefficients, parts, block):
    height = coefficients.shape[0]
    shape = jax.ShapeDtypeStruct((height, CAP_B * block), coefficients.dtype)
    return pl.pallas_call(
        functools.partial(pack_beta_body, block),
        grid_spec=pltpu.PrefetchScalarGridSpec(
            num_scalar_prefetch=1,
            grid=(),
            in_specs=[pl.BlockSpec(memory_space=pltpu.VMEM)],
            out_specs=[pl.BlockSpec(memory_space=pltpu.VMEM)] * parts,
        ),
        out_shape=[shape] * parts,
        compiler_params=pltpu.CompilerParams(vmem_limit_bytes=VMEM_LIMIT),
        name="pack_beta",
    )(pack, coefficients)


def fill(weights, table_ref, h_ref, rows, positions, block):
    for i in range(rows):
        for q in range(positions):
            k = table_ref[i * positions + q]
            tile = h_ref[i, jnp.maximum(k, 0)]
            weights[i * block : (i + 1) * block, q * block : (q + 1) * block] = jnp.where(
                k >= 0, tile, jnp.zeros_like(tile)
            )


def beta_body(rows, positions, block, table_ref, h_ref, d_ref, c_ref, *rest):
    arrived, out_ref, weights = rest[:-2], rest[-2], rest[-1]
    fill(weights, table_ref, h_ref, rows, positions, block)
    own = c_ref[...]
    x = jnp.concatenate([own] + [a[...] for a in arrived], axis=1)
    total = lax.dot_general(
        x, weights[...], (((1,), (1,)), ((), ())), preferred_element_type=jnp.float32
    )
    out_ref[...] = total + d_ref[...] * own.astype(jnp.float32)


def beta_product(table, beta_blocks, coefficients, diagonal, arrived):
    rows, block = beta_blocks.shape[0], beta_blocks.shape[2]
    positions = table.shape[1]
    return pl.pallas_call(
        functools.partial(beta_body, rows, positions, block),
        grid_spec=pltpu.PrefetchScalarGridSpec(
            num_scalar_prefetch=1,
            grid=(),
            in_specs=[pl.BlockSpec(memory_space=pltpu.VMEM)] * (3 + len(arrived)),
            out_specs=pl.BlockSpec(memory_space=pltpu.VMEM),
            scratch_shapes=[pltpu.VMEM((rows * block, positions * block), jnp.bfloat16)],
        ),
        out_shape=jax.ShapeDtypeStruct(diagonal.shape, jnp.float32),
        compiler_params=pltpu.CompilerParams(vmem_limit_bytes=VMEM_LIMIT),
        name="beta_product",
    )(table.reshape(-1), beta_blocks, diagonal, coefficients, *arrived)


def lay_out(table, blocks):
    rows, block = blocks.shape[0], blocks.shape[2]
    positions = table.shape[1]

    def body(table_ref, h_ref, out_ref):
        fill(out_ref, table_ref, h_ref, rows, positions, block)

    return pl.pallas_call(
        body,
        grid_spec=pltpu.PrefetchScalarGridSpec(
            num_scalar_prefetch=1,
            grid=(),
            in_specs=[pl.BlockSpec(memory_space=pltpu.VMEM)],
            out_specs=pl.BlockSpec(memory_space=pltpu.VMEM),
        ),
        out_shape=jax.ShapeDtypeStruct((rows * block, positions * block), blocks.dtype),
        compiler_params=pltpu.CompilerParams(vmem_limit_bytes=VMEM_LIMIT),
        name="lay_out",
    )(table.reshape(-1), blocks)


def alpha_product(weights, pieces, acc, dtype):
    def body(w_ref, acc_ref, *rest):
        x = jnp.concatenate([p[...] for p in rest[:-1]], axis=0)
        total = acc_ref[...] + jnp.dot(w_ref[...], x, preferred_element_type=jnp.float32)
        rest[-1][...] = total.astype(dtype)

    return pl.pallas_call(
        body,
        in_specs=[pl.BlockSpec(memory_space=pltpu.VMEM)] * (2 + len(pieces)),
        out_specs=pl.BlockSpec(memory_space=pltpu.VMEM),
        out_shape=jax.ShapeDtypeStruct(acc.shape, dtype),
        compiler_params=pltpu.CompilerParams(vmem_limit_bytes=VMEM_LIMIT),
        name="alpha_product",
    )(weights, acc, *pieces)


def send(x, edges):
    return lax.ppermute(x, "alpha", [(s * CORES + c, t * CORES + c) for s, t in edges for c in range(CORES)])


def swap(x, chips):
    return lax.ppermute(x, "alpha", [(p * CORES + c, p * CORES + 1 - c) for p in chips for c in range(CORES)])


def gate(*values):
    return lax.optimization_barrier(values)


def block_ids(places, rows):
    ids = np.full((len(places), CORES, len(places[0])), -1, np.int32)
    for p, line in enumerate(places):
        for g, place in enumerate(line):
            if place is not None:
                for c in range(CORES):
                    ids[p, c, g] = (place[0] * CORES + c) * rows + place[1]
    return ids


def per_device(coefficients, diagonal, alpha_blocks, alpha_lists, beta_blocks, beta_lists):
    block = alpha_blocks.shape[2]
    rows_a, rows_b = alpha_blocks.shape[0], beta_blocks.shape[0]
    chips = lax.axis_size("alpha") // CORES
    owners_b = lax.axis_size("beta")
    index_a, index_b = lax.axis_index("alpha"), lax.axis_index("beta")

    pack, beta_ids = beta_tables(beta_lists, index_b, owners_b, rows_b)
    mine_b = lax.dynamic_slice_in_dim(beta_lists, index_b * rows_b, rows_b, 0)

    def place(chip, first, count):
        return [(chip, first + g) if 0 <= chip < chips else None for g in range(count)]

    mine_a = lax.dynamic_slice_in_dim(alpha_lists, index_a * rows_a, rows_a, 0)

    def table_of(places):
        ids = [block_ids(p, rows_a) for p in places]
        ids = jnp.asarray(np.concatenate(ids + [i[:, ::-1] for i in ids], axis=2).reshape(chips * CORES, -1))
        return slot_table(mine_a, lax.dynamic_index_in_dim(ids, index_a, 0, keepdims=False))

    table_b = slot_table(mine_b, beta_ids)

    def beta_all(arrived):
        return beta_product(table_b, beta_blocks, coefficients, diagonal, arrived)

    def exchange(packed):
        steps = range(1, owners_b)
        return [
            lax.ppermute(packed[s - 1], "beta", [(d, partner(d, s, owners_b)) for d in range(owners_b)]) for s in steps
        ]

    everyone = range(chips)
    own = [place(p, 0, rows_a) for p in everyone]
    if chips == 4:
        far, near = [(0, 2), (1, 3), (2, 0), (3, 1)], [(0, 1), (1, 0), (2, 3), (3, 2)]
        far_from, near_from, both_from = [2, 3, 0, 1], [1, 0, 3, 2], [3, 2, 1, 0]


        def of(chip_of):
            return [place(chip_of[p], 0, rows_a) for p in everyone]

        table_here = table_of([own, of(near_from), of(far_from)])
        table_both = table_of([of(both_from)])
        half = table_both.shape[1] // 2

        near_own, far_own = send(coefficients, near), send(coefficients, far)
        arrived = exchange(pack_beta(pack, coefficients, owners_b - 1, block))
        own_swapped = swap(coefficients, everyone)
        near_own, far_own, own_swapped, here, table_here, table_b, table_same, table_other, *arrived = gate(
            near_own, far_own, own_swapped, coefficients, table_here, table_b, table_both[:, :half], table_both[:, half:], *arrived
        )

        near_far = send(far_own, near)
        pieces = [here, near_own, far_own]
        pieces += [own_swapped, swap(near_own, everyone), swap(far_own, everyone)]
        *pieces, here, blocks_here = gate(*pieces, here, alpha_blocks)
        acc = beta_product(table_b, beta_blocks, here, diagonal, arrived)
        weights = [lay_out(table, blocks_here) for table in (table_here, table_same, table_other)]
        acc = alpha_product(weights[0], pieces, acc, jnp.float32)
        near_far, acc, *weights = gate(near_far, acc, *weights)
        acc = alpha_product(weights[1], [near_far], acc, jnp.float32)
        return alpha_product(weights[2], [swap(near_far, everyone)], acc, jnp.bfloat16)

    arrived = exchange(pack_beta(pack, coefficients, owners_b - 1, block))
    pieces, places = [coefficients], [own]
    left, right = [], []
    for u in range((chips - 1) * rows_a):
        kind, v = u // rows_a, u % rows_a
        mine = coefficients[v * block : (v + 1) * block]
        left.append(send(mine if u < rows_a else left[u - rows_a], [(p, p - 1) for p in range(1, chips) if kind < chips - p]))
        right.append(send(mine if u < rows_a else right[u - rows_a], [(p, p + 1) for p in range(chips - 1) if kind < p + 1]))
        pieces += [left[u], right[u]]
        places += [[place(p + 1 + kind, v, 1) for p in everyone], [place(p - 1 - kind, v, 1) for p in everyone]]
    acc = beta_product(table_b, beta_blocks, coefficients, diagonal, arrived)
    step = 2 * rows_a
    for k in range(0, len(pieces), step):
        last = k + step >= len(pieces)
        weights = lay_out(table_of(places[k : k + step]), alpha_blocks)
        xs = pieces[k : k + step] + [swap(x, everyone) for x in pieces[k : k + step]]
        acc = alpha_product(weights, xs, acc, jnp.bfloat16 if last else jnp.float32)
    return acc


def solution(mesh):
    in_specs = (
        P("alpha", "beta"),
        P("alpha", "beta"),
        P("alpha", None, None, None),
        P(),
        P("beta", None, None, None),
        P(),
    )
    out_specs = P("alpha", "beta")
    return jax.shard_map(
        per_device, mesh=mesh, in_specs=in_specs, out_specs=out_specs, check_vma=False
    )
```

```python
import functools

import jax
import jax.numpy as jnp
import numpy as np
from jax import lax
from jax.experimental import pallas as pl
from jax.experimental.pallas import tpu as pltpu
from jax.sharding import PartitionSpec as P

CAP_B = 4
CORES = 2
FIRST = 1
VMEM_LIMIT = 40 * 1024 * 1024


def beta_tables(beta_lists, me, owners, per_owner):
    number = owners * per_owner
    ids = jnp.arange(number, dtype=jnp.int32)
    flat = beta_lists.reshape(owners, -1)
    needed = jnp.any(flat[:, :, None] == ids, axis=1)
    same = (ids[:, None] // per_owner == ids[None, :] // per_owner) & (ids[:, None] < ids[None, :])
    rank = jnp.sum((needed[:, :, None] & same).astype(jnp.int32), axis=1)
    caps = jnp.arange(CAP_B, dtype=jnp.int32)
    match = needed[:, :, None] & (rank[:, :, None] == caps)
    match = match.reshape(owners, owners, per_owner, CAP_B)
    local = jnp.arange(per_owner, dtype=jnp.int32)[:, None]
    chosen = jnp.max(jnp.where(match, local, -1), axis=2)
    pack = lax.dynamic_index_in_dim(chosen, me, 1, keepdims=False)
    got = lax.dynamic_index_in_dim(chosen, me, 0, keepdims=False)
    got = jnp.where(got >= 0, got + jnp.arange(owners, dtype=jnp.int32)[:, None] * per_owner, -1)
    return jnp.maximum(pack, 0).reshape(-1), got.reshape(-1)


def slot_table(lists, position_ids):
    slots = jnp.arange(lists.shape[1], dtype=jnp.int32)[None, :, None]
    hit = lists[:, :, None] == position_ids[None, None, :]
    return jnp.max(jnp.where(hit, slots, -1), axis=1)


def pack_beta(pack, coefficients, parts, block):
    height = coefficients.shape[0]

    def body(pack_ref, c_ref, out_ref):
        for s in range(parts):
            for c in range(CAP_B):
                j = pack_ref[s * CAP_B + c]
                column = pl.ds(pl.multiple_of(j * block, block), block)
                out_ref[s, :, c * block : (c + 1) * block] = c_ref[:, column]

    return pl.pallas_call(
        body,
        grid_spec=pltpu.PrefetchScalarGridSpec(
            num_scalar_prefetch=1,
            grid=(),
            in_specs=[pl.BlockSpec(memory_space=pltpu.VMEM)],
            out_specs=pl.BlockSpec(memory_space=pltpu.VMEM),
        ),
        out_shape=jax.ShapeDtypeStruct((parts, height, CAP_B * block), coefficients.dtype),
        compiler_params=pltpu.CompilerParams(vmem_limit_bytes=VMEM_LIMIT),
        name="pack_beta",
    )(pack, coefficients)


def fill(weights, table_ref, h_ref, rows, positions, block):
    for i in range(rows):
        for q in range(positions):
            k = table_ref[i * positions + q]
            tile = h_ref[i, jnp.maximum(k, 0)]
            weights[i * block : (i + 1) * block, q * block : (q + 1) * block] = jnp.where(
                k >= 0, tile, jnp.zeros_like(tile)
            )


def beta_product(table, beta_blocks, coefficients, diagonal, arrived):
    rows, block = beta_blocks.shape[0], beta_blocks.shape[2]
    parts, positions = arrived.shape[0], table.shape[1]

    def body(table_ref, h_ref, d_ref, c_ref, x_ref, out_ref, weights):
        fill(weights, table_ref, h_ref, rows, positions, block)
        x = jnp.concatenate([x_ref[s] for s in range(parts)], axis=1)
        total = lax.dot_general(
            x, weights[...], (((1,), (1,)), ((), ())), preferred_element_type=jnp.float32
        )
        out_ref[...] = total + d_ref[...] * c_ref[...].astype(jnp.float32)

    return pl.pallas_call(
        body,
        grid_spec=pltpu.PrefetchScalarGridSpec(
            num_scalar_prefetch=1,
            grid=(),
            in_specs=[pl.BlockSpec(memory_space=pltpu.VMEM)] * 4,
            out_specs=pl.BlockSpec(memory_space=pltpu.VMEM),
            scratch_shapes=[pltpu.VMEM((rows * block, positions * block), jnp.bfloat16)],
        ),
        out_shape=jax.ShapeDtypeStruct(diagonal.shape, jnp.float32),
        compiler_params=pltpu.CompilerParams(vmem_limit_bytes=VMEM_LIMIT),
        name="beta_product",
    )(table.reshape(-1), beta_blocks, diagonal, coefficients, arrived)


def lay_out(table, blocks):
    rows, block = blocks.shape[0], blocks.shape[2]
    positions = table.shape[1]

    def body(table_ref, h_ref, out_ref):
        fill(out_ref, table_ref, h_ref, rows, positions, block)

    return pl.pallas_call(
        body,
        grid_spec=pltpu.PrefetchScalarGridSpec(
            num_scalar_prefetch=1,
            grid=(),
            in_specs=[pl.BlockSpec(memory_space=pltpu.VMEM)],
            out_specs=pl.BlockSpec(memory_space=pltpu.VMEM),
        ),
        out_shape=jax.ShapeDtypeStruct((rows * block, positions * block), blocks.dtype),
        compiler_params=pltpu.CompilerParams(vmem_limit_bytes=VMEM_LIMIT),
        name="lay_out",
    )(table.reshape(-1), blocks)


def alpha_product(weights, pieces, acc, dtype):
    def body(w_ref, acc_ref, *rest):
        x = jnp.concatenate([p[...] for p in rest[:-1]], axis=0)
        total = acc_ref[...] + jnp.dot(w_ref[...], x, preferred_element_type=jnp.float32)
        rest[-1][...] = total.astype(dtype)

    return pl.pallas_call(
        body,
        in_specs=[pl.BlockSpec(memory_space=pltpu.VMEM)] * (2 + len(pieces)),
        out_specs=pl.BlockSpec(memory_space=pltpu.VMEM),
        out_shape=jax.ShapeDtypeStruct(acc.shape, dtype),
        compiler_params=pltpu.CompilerParams(vmem_limit_bytes=VMEM_LIMIT),
        name="alpha_product",
    )(weights, acc, *pieces)


def send(x, edges):
    return lax.ppermute(x, "alpha", [(s * CORES + c, t * CORES + c) for s, t in edges for c in range(CORES)])


def swap(x, chips):
    return lax.ppermute(x, "alpha", [(p * CORES + c, p * CORES + 1 - c) for p in chips for c in range(CORES)])


def gate(*values):
    return lax.optimization_barrier(values)


def block_ids(places, rows):
    ids = np.full((len(places), CORES, len(places[0])), -1, np.int32)
    for p, line in enumerate(places):
        for g, place in enumerate(line):
            if place is not None:
                for c in range(CORES):
                    ids[p, c, g] = (place[0] * CORES + c) * rows + place[1]
    return ids


def per_device(coefficients, diagonal, alpha_blocks, alpha_lists, beta_blocks, beta_lists):
    block = alpha_blocks.shape[2]
    rows_a, rows_b = alpha_blocks.shape[0], beta_blocks.shape[0]
    chips = lax.axis_size("alpha") // CORES
    owners_b = lax.axis_size("beta")
    index_a, index_b = lax.axis_index("alpha"), lax.axis_index("beta")

    pack, beta_ids = beta_tables(beta_lists, index_b, owners_b, rows_b)
    mine_b = lax.dynamic_slice_in_dim(beta_lists, index_b * rows_b, rows_b, 0)

    def place(chip, first, count):
        return [(chip, first + g) if 0 <= chip < chips else None for g in range(count)]

    mine_a = lax.dynamic_slice_in_dim(alpha_lists, index_a * rows_a, rows_a, 0)

    def table_of(places):
        ids = [block_ids(p, rows_a) for p in places]
        ids = jnp.asarray(np.concatenate(ids + [i[:, ::-1] for i in ids], axis=2).reshape(chips * CORES, -1))
        return slot_table(mine_a, lax.dynamic_index_in_dim(ids, index_a, 0, keepdims=False))

    table_b = slot_table(mine_b, beta_ids)

    def beta_all(arrived):
        return beta_product(table_b, beta_blocks, coefficients, diagonal, arrived)

    def exchange():
        packed = pack_beta(pack, coefficients, owners_b, block)
        return lax.all_to_all(packed, "beta", split_axis=0, concat_axis=0, tiled=True)

    everyone = range(chips)
    own = [place(p, 0, rows_a) for p in everyone]
    if chips == 4:
        far, near = [(0, 2), (1, 3), (2, 0), (3, 1)], [(0, 1), (1, 0), (2, 3), (3, 2)]
        far_from, near_from, both_from = [2, 3, 0, 1], [1, 0, 3, 2], [3, 2, 1, 0]


        cuts = [(0, FIRST), (FIRST, rows_a - FIRST)]

        def of(chip_of, first=0, count=rows_a):
            return [place(chip_of[p], first, count) for p in everyone]

        table_here = table_of([own, of(near_from)] + [of(far_from, *cut) for cut in cuts] + [of(both_from, *cuts[0])])
        table_last = table_of([of(both_from, *cuts[1])])
        half = table_last.shape[1] // 2
        tables = (table_here, table_last[:, :half], table_last[:, half:])

        far_own = [send(coefficients[f * block : (f + n) * block], far) for f, n in cuts]
        near_own = send(coefficients, near)
        near_far = send(far_own[0], near)
        own_swapped = swap(coefficients, everyone)
        arrived = exchange()
        near_far, near_own, far_own[1], own_swapped, here, table_b, *tables = gate(
            near_far, near_own, far_own[1], own_swapped, coefficients, table_b, *tables
        )
        near_last = send(far_own[1], near)
        pieces = [here, near_own, *far_own, near_far]
        pieces += [own_swapped] + [swap(x, everyone) for x in pieces[1:]]
        *pieces, here, blocks_here, arrived = gate(*pieces, here, alpha_blocks, arrived)
        weights = [lay_out(table, blocks_here) for table in tables]
        acc = beta_product(table_b, beta_blocks, here, diagonal, arrived)
        acc = alpha_product(weights[0], pieces, acc, jnp.float32)
        near_last, acc, *weights = gate(near_last, acc, *weights)
        acc = alpha_product(weights[1], [near_last], acc, jnp.float32)
        return alpha_product(weights[2], [swap(near_last, everyone)], acc, jnp.bfloat16)

    arrived = exchange()
    pieces, places = [coefficients], [own]
    left, right = [], []
    for u in range((chips - 1) * rows_a):
        kind, v = u // rows_a, u % rows_a
        mine = coefficients[v * block : (v + 1) * block]
        left.append(send(mine if u < rows_a else left[u - rows_a], [(p, p - 1) for p in range(1, chips) if kind < chips - p]))
        right.append(send(mine if u < rows_a else right[u - rows_a], [(p, p + 1) for p in range(chips - 1) if kind < p + 1]))
        pieces += [left[u], right[u]]
        places += [[place(p + 1 + kind, v, 1) for p in everyone], [place(p - 1 - kind, v, 1) for p in everyone]]
    acc = beta_product(table_b, beta_blocks, coefficients, diagonal, arrived)
    step = 2 * rows_a
    for k in range(0, len(pieces), step):
        last = k + step >= len(pieces)
        weights = lay_out(table_of(places[k : k + step]), alpha_blocks)
        xs = pieces[k : k + step] + [swap(x, everyone) for x in pieces[k : k + step]]
        acc = alpha_product(weights, xs, acc, jnp.bfloat16 if last else jnp.float32)
    return acc


def solution(mesh):
    in_specs = (
        P("alpha", "beta"),
        P("alpha", "beta"),
        P("alpha", None, None, None),
        P(),
        P("beta", None, None, None),
        P(),
    )
    out_specs = P("alpha", "beta")
    return jax.shard_map(
        per_device, mesh=mesh, in_specs=in_specs, out_specs=out_specs, check_vma=False
    )
```

```python
import functools

import jax
import jax.numpy as jnp
import numpy as np
from jax import lax
from jax.experimental import pallas as pl
from jax.experimental.pallas import tpu as pltpu
from jax.sharding import PartitionSpec as P

CAP_B = 4
CORES = 2
FIRST = 1
VMEM_LIMIT = 40 * 1024 * 1024


def beta_tables(beta_lists, me, owners, per_owner):
    number = owners * per_owner
    ids = jnp.arange(number, dtype=jnp.int32)
    flat = beta_lists.reshape(owners, -1)
    needed = jnp.any(flat[:, :, None] == ids, axis=1)
    same = (ids[:, None] // per_owner == ids[None, :] // per_owner) & (ids[:, None] < ids[None, :])
    rank = jnp.sum((needed[:, :, None] & same).astype(jnp.int32), axis=1)
    caps = jnp.arange(CAP_B, dtype=jnp.int32)
    match = needed[:, :, None] & (rank[:, :, None] == caps)
    match = match.reshape(owners, owners, per_owner, CAP_B)
    local = jnp.arange(per_owner, dtype=jnp.int32)[:, None]
    chosen = jnp.max(jnp.where(match, local, -1), axis=2)
    pack = lax.dynamic_index_in_dim(chosen, me, 1, keepdims=False)
    got = lax.dynamic_index_in_dim(chosen, me, 0, keepdims=False)
    got = jnp.where(got >= 0, got + jnp.arange(owners, dtype=jnp.int32)[:, None] * per_owner, -1)
    return jnp.maximum(pack, 0).reshape(-1), got.reshape(-1)


def slot_table(lists, position_ids):
    slots = jnp.arange(lists.shape[1], dtype=jnp.int32)[None, :, None]
    hit = lists[:, :, None] == position_ids[None, None, :]
    return jnp.max(jnp.where(hit, slots, -1), axis=1)


def pack_beta(pack, coefficients, parts, block):
    height = coefficients.shape[0]

    def body(pack_ref, c_ref, out_ref):
        for s in range(parts):
            for c in range(CAP_B):
                j = pack_ref[s * CAP_B + c]
                column = pl.ds(pl.multiple_of(j * block, block), block)
                out_ref[s, :, c * block : (c + 1) * block] = c_ref[:, column]

    return pl.pallas_call(
        body,
        grid_spec=pltpu.PrefetchScalarGridSpec(
            num_scalar_prefetch=1,
            grid=(),
            in_specs=[pl.BlockSpec(memory_space=pltpu.VMEM)],
            out_specs=pl.BlockSpec(memory_space=pltpu.VMEM),
        ),
        out_shape=jax.ShapeDtypeStruct((parts, height, CAP_B * block), coefficients.dtype),
        compiler_params=pltpu.CompilerParams(vmem_limit_bytes=VMEM_LIMIT),
        name="pack_beta",
    )(pack, coefficients)


def fill(weights, table_ref, h_ref, rows, positions, block):
    for i in range(rows):
        for q in range(positions):
            k = table_ref[i * positions + q]
            tile = h_ref[i, jnp.maximum(k, 0)]
            weights[i * block : (i + 1) * block, q * block : (q + 1) * block] = jnp.where(
                k >= 0, tile, jnp.zeros_like(tile)
            )


def beta_product(table, beta_blocks, coefficients, diagonal, arrived, acc):
    rows, block = beta_blocks.shape[0], beta_blocks.shape[2]
    parts, positions = arrived.shape[0], table.shape[1]

    def body(table_ref, h_ref, d_ref, c_ref, x_ref, acc_ref, out_ref, weights):
        fill(weights, table_ref, h_ref, rows, positions, block)
        x = jnp.concatenate([x_ref[s] for s in range(parts)], axis=1)
        total = lax.dot_general(
            x, weights[...], (((1,), (1,)), ((), ())), preferred_element_type=jnp.float32
        )
        out_ref[...] = acc_ref[...] + total + d_ref[...] * c_ref[...].astype(jnp.float32)

    return pl.pallas_call(
        body,
        grid_spec=pltpu.PrefetchScalarGridSpec(
            num_scalar_prefetch=1,
            grid=(),
            in_specs=[pl.BlockSpec(memory_space=pltpu.VMEM)] * 5,
            out_specs=pl.BlockSpec(memory_space=pltpu.VMEM),
            scratch_shapes=[pltpu.VMEM((rows * block, positions * block), jnp.bfloat16)],
        ),
        out_shape=jax.ShapeDtypeStruct(diagonal.shape, jnp.float32),
        compiler_params=pltpu.CompilerParams(vmem_limit_bytes=VMEM_LIMIT),
        name="beta_product",
    )(table.reshape(-1), beta_blocks, diagonal, coefficients, arrived, acc)


def lay_out(table, blocks):
    rows, block = blocks.shape[0], blocks.shape[2]
    positions = table.shape[1]

    def body(table_ref, h_ref, out_ref):
        fill(out_ref, table_ref, h_ref, rows, positions, block)

    return pl.pallas_call(
        body,
        grid_spec=pltpu.PrefetchScalarGridSpec(
            num_scalar_prefetch=1,
            grid=(),
            in_specs=[pl.BlockSpec(memory_space=pltpu.VMEM)],
            out_specs=pl.BlockSpec(memory_space=pltpu.VMEM),
        ),
        out_shape=jax.ShapeDtypeStruct((rows * block, positions * block), blocks.dtype),
        compiler_params=pltpu.CompilerParams(vmem_limit_bytes=VMEM_LIMIT),
        name="lay_out",
    )(table.reshape(-1), blocks)


def alpha_product(weights, pieces, acc, dtype):
    adds = [] if acc is None else [acc]

    def body(w_ref, *rest):
        x = jnp.concatenate([p[...] for p in rest[len(adds) : -1]], axis=0)
        total = jnp.dot(w_ref[...], x, preferred_element_type=jnp.float32)
        if adds:
            total = rest[0][...] + total
        rest[-1][...] = total.astype(dtype)

    return pl.pallas_call(
        body,
        in_specs=[pl.BlockSpec(memory_space=pltpu.VMEM)] * (1 + len(adds) + len(pieces)),
        out_specs=pl.BlockSpec(memory_space=pltpu.VMEM),
        out_shape=jax.ShapeDtypeStruct((weights.shape[0], pieces[0].shape[1]), dtype),
        compiler_params=pltpu.CompilerParams(vmem_limit_bytes=VMEM_LIMIT),
        name="alpha_product",
    )(weights, *adds, *pieces)


def send(x, edges):
    return lax.ppermute(x, "alpha", [(s * CORES + c, t * CORES + c) for s, t in edges for c in range(CORES)])


def swap(x, chips):
    return lax.ppermute(x, "alpha", [(p * CORES + c, p * CORES + 1 - c) for p in chips for c in range(CORES)])


def gate(*values):
    return lax.optimization_barrier(values)


def block_ids(places, rows):
    ids = np.full((len(places), CORES, len(places[0])), -1, np.int32)
    for p, line in enumerate(places):
        for g, place in enumerate(line):
            if place is not None:
                for c in range(CORES):
                    ids[p, c, g] = (place[0] * CORES + c) * rows + place[1]
    return ids


def per_device(coefficients, diagonal, alpha_blocks, alpha_lists, beta_blocks, beta_lists):
    block = alpha_blocks.shape[2]
    rows_a, rows_b = alpha_blocks.shape[0], beta_blocks.shape[0]
    chips = lax.axis_size("alpha") // CORES
    owners_b = lax.axis_size("beta")
    index_a, index_b = lax.axis_index("alpha"), lax.axis_index("beta")

    pack, beta_ids = beta_tables(beta_lists, index_b, owners_b, rows_b)
    mine_b = lax.dynamic_slice_in_dim(beta_lists, index_b * rows_b, rows_b, 0)

    def place(chip, first, count):
        return [(chip, first + g) if 0 <= chip < chips else None for g in range(count)]

    mine_a = lax.dynamic_slice_in_dim(alpha_lists, index_a * rows_a, rows_a, 0)

    def table_of(places):
        ids = [block_ids(p, rows_a) for p in places]
        ids = jnp.asarray(np.concatenate(ids + [i[:, ::-1] for i in ids], axis=2).reshape(chips * CORES, -1))
        return slot_table(mine_a, lax.dynamic_index_in_dim(ids, index_a, 0, keepdims=False))

    table_b = slot_table(mine_b, beta_ids)

    def exchange():
        packed = pack_beta(pack, coefficients, owners_b, block)
        return lax.all_to_all(packed, "beta", split_axis=0, concat_axis=0, tiled=True)

    everyone = range(chips)
    own = [place(p, 0, rows_a) for p in everyone]
    if chips == 4:
        far, near = [(0, 2), (1, 3), (2, 0), (3, 1)], [(0, 1), (1, 0), (2, 3), (3, 2)]
        far_from, near_from, both_from = [2, 3, 0, 1], [1, 0, 3, 2], [3, 2, 1, 0]


        cuts = [(0, FIRST), (FIRST, rows_a - FIRST)]

        def of(chip_of, first=0, count=rows_a):
            return [place(chip_of[p], first, count) for p in everyone]

        table_here = table_of([own, of(near_from)] + [of(far_from, *cut) for cut in cuts] + [of(both_from, *cuts[0])])
        table_last = table_of([of(both_from, *cuts[1])])
        half = table_last.shape[1] // 2
        tables = (table_here, table_last[:, :half], table_last[:, half:])

        far_own = [send(coefficients[f * block : (f + n) * block], far) for f, n in cuts]
        near_own = send(coefficients, near)
        near_far = send(far_own[0], near)
        own_swapped = swap(coefficients, everyone)
        arrived = exchange()
        weights = [lay_out(table, alpha_blocks) for table in tables]
        near_far, far_own[1], here, table_b, *weights = gate(near_far, far_own[1], coefficients, table_b, *weights)
        near_last = send(far_own[1], near)
        pieces = [here, near_own, *far_own, near_far]
        pieces += [own_swapped] + [swap(x, everyone) for x in pieces[1:]]
        *pieces, here, arrived = gate(*pieces, here, arrived)
        acc = alpha_product(weights[0], pieces, None, jnp.float32)
        acc = beta_product(table_b, beta_blocks, here, diagonal, arrived, acc)
        near_last, acc = gate(near_last, acc)
        acc = alpha_product(weights[1], [near_last], acc, jnp.float32)
        return alpha_product(weights[2], [swap(near_last, everyone)], acc, jnp.bfloat16)

    arrived = exchange()
    pieces, places = [coefficients], [own]
    left, right = [], []
    for u in range((chips - 1) * rows_a):
        kind, v = u // rows_a, u % rows_a
        mine = coefficients[v * block : (v + 1) * block]
        left.append(send(mine if u < rows_a else left[u - rows_a], [(p, p - 1) for p in range(1, chips) if kind < chips - p]))
        right.append(send(mine if u < rows_a else right[u - rows_a], [(p, p + 1) for p in range(chips - 1) if kind < p + 1]))
        pieces += [left[u], right[u]]
        places += [[place(p + 1 + kind, v, 1) for p in everyone], [place(p - 1 - kind, v, 1) for p in everyone]]
    acc = jnp.zeros(diagonal.shape, jnp.float32)
    acc = beta_product(table_b, beta_blocks, coefficients, diagonal, arrived, acc)
    step = 2 * rows_a
    for k in range(0, len(pieces), step):
        last = k + step >= len(pieces)
        weights = lay_out(table_of(places[k : k + step]), alpha_blocks)
        xs = pieces[k : k + step] + [swap(x, everyone) for x in pieces[k : k + step]]
        acc = alpha_product(weights, xs, acc, jnp.bfloat16 if last else jnp.float32)
    return acc


def solution(mesh):
    in_specs = (
        P("alpha", "beta"),
        P("alpha", "beta"),
        P("alpha", None, None, None),
        P(),
        P("beta", None, None, None),
        P(),
    )
    out_specs = P("alpha", "beta")
    return jax.shard_map(
        per_device, mesh=mesh, in_specs=in_specs, out_specs=out_specs, check_vma=False
    )
```

```python
import functools

import jax
import jax.numpy as jnp
import numpy as np
from jax import lax
from jax.experimental import pallas as pl
from jax.experimental.pallas import tpu as pltpu
from jax.sharding import PartitionSpec as P

CAP_B = 4
CORES = 2
FIRST = 1
VMEM_LIMIT = 40 * 1024 * 1024


def beta_tables(beta_lists, me, owners, per_owner):
    number = owners * per_owner
    ids = jnp.arange(number, dtype=jnp.int32)
    flat = beta_lists.reshape(owners, -1)
    needed = jnp.any(flat[:, :, None] == ids, axis=1)
    same = (ids[:, None] // per_owner == ids[None, :] // per_owner) & (ids[:, None] < ids[None, :])
    rank = jnp.sum((needed[:, :, None] & same).astype(jnp.int32), axis=1)
    caps = jnp.arange(CAP_B, dtype=jnp.int32)
    match = needed[:, :, None] & (rank[:, :, None] == caps)
    match = match.reshape(owners, owners, per_owner, CAP_B)
    local = jnp.arange(per_owner, dtype=jnp.int32)[:, None]
    chosen = jnp.max(jnp.where(match, local, -1), axis=2)
    pack = lax.dynamic_index_in_dim(chosen, me, 1, keepdims=False)
    got = lax.dynamic_index_in_dim(chosen, me, 0, keepdims=False)
    got = jnp.where(got >= 0, got + jnp.arange(owners, dtype=jnp.int32)[:, None] * per_owner, -1)
    return jnp.maximum(pack, 0).reshape(-1), got.reshape(-1)


def slot_table(lists, position_ids):
    slots = jnp.arange(lists.shape[1], dtype=jnp.int32)[None, :, None]
    hit = lists[:, :, None] == position_ids[None, None, :]
    return jnp.max(jnp.where(hit, slots, -1), axis=1)


def pack_beta(pack, coefficients, parts, block):
    height = coefficients.shape[0]

    def body(pack_ref, c_ref, out_ref):
        for s in range(parts):
            for c in range(CAP_B):
                j = pack_ref[s * CAP_B + c]
                column = pl.ds(pl.multiple_of(j * block, block), block)
                out_ref[s, :, c * block : (c + 1) * block] = c_ref[:, column]

    return pl.pallas_call(
        body,
        grid_spec=pltpu.PrefetchScalarGridSpec(
            num_scalar_prefetch=1,
            grid=(),
            in_specs=[pl.BlockSpec(memory_space=pltpu.VMEM)],
            out_specs=pl.BlockSpec(memory_space=pltpu.VMEM),
        ),
        out_shape=jax.ShapeDtypeStruct((parts, height, CAP_B * block), coefficients.dtype),
        compiler_params=pltpu.CompilerParams(vmem_limit_bytes=VMEM_LIMIT),
        name="pack_beta",
    )(pack, coefficients)


def fill(weights, table_ref, h_ref, rows, positions, block):
    for i in range(rows):
        for q in range(positions):
            k = table_ref[i * positions + q]
            tile = h_ref[i, jnp.maximum(k, 0)]
            weights[i * block : (i + 1) * block, q * block : (q + 1) * block] = jnp.where(
                k >= 0, tile, jnp.zeros_like(tile)
            )


def beta_product(table, beta_blocks, coefficients, diagonal, arrived, acc):
    rows, block = beta_blocks.shape[0], beta_blocks.shape[2]
    parts, positions = arrived.shape[0], table.shape[1]

    def body(table_ref, h_ref, d_ref, c_ref, x_ref, acc_ref, out_ref, weights):
        fill(weights, table_ref, h_ref, rows, positions, block)
        x = jnp.concatenate([x_ref[s] for s in range(parts)], axis=1)
        total = lax.dot_general(
            x, weights[...], (((1,), (1,)), ((), ())), preferred_element_type=jnp.float32
        )
        out_ref[...] = acc_ref[...] + total + d_ref[...] * c_ref[...].astype(jnp.float32)

    return pl.pallas_call(
        body,
        grid_spec=pltpu.PrefetchScalarGridSpec(
            num_scalar_prefetch=1,
            grid=(),
            in_specs=[pl.BlockSpec(memory_space=pltpu.VMEM)] * 5,
            out_specs=pl.BlockSpec(memory_space=pltpu.VMEM),
            scratch_shapes=[pltpu.VMEM((rows * block, positions * block), jnp.bfloat16)],
        ),
        out_shape=jax.ShapeDtypeStruct(diagonal.shape, jnp.float32),
        compiler_params=pltpu.CompilerParams(vmem_limit_bytes=VMEM_LIMIT),
        name="beta_product",
    )(table.reshape(-1), beta_blocks, diagonal, coefficients, arrived, acc)


def lay_out(table, blocks):
    rows, block = blocks.shape[0], blocks.shape[2]
    positions = table.shape[1]

    def body(table_ref, h_ref, out_ref):
        fill(out_ref, table_ref, h_ref, rows, positions, block)

    return pl.pallas_call(
        body,
        grid_spec=pltpu.PrefetchScalarGridSpec(
            num_scalar_prefetch=1,
            grid=(),
            in_specs=[pl.BlockSpec(memory_space=pltpu.VMEM)],
            out_specs=pl.BlockSpec(memory_space=pltpu.VMEM),
        ),
        out_shape=jax.ShapeDtypeStruct((rows * block, positions * block), blocks.dtype),
        compiler_params=pltpu.CompilerParams(vmem_limit_bytes=VMEM_LIMIT),
        name="lay_out",
    )(table.reshape(-1), blocks)


def alpha_product(weights, pieces, acc, dtype):
    adds = [] if acc is None else [acc]

    def body(w_ref, *rest):
        x = jnp.concatenate([p[...] for p in rest[len(adds) : -1]], axis=0)
        total = jnp.dot(w_ref[...], x, preferred_element_type=jnp.float32)
        if adds:
            total = rest[0][...] + total
        rest[-1][...] = total.astype(dtype)

    return pl.pallas_call(
        body,
        in_specs=[pl.BlockSpec(memory_space=pltpu.VMEM)] * (1 + len(adds) + len(pieces)),
        out_specs=pl.BlockSpec(memory_space=pltpu.VMEM),
        out_shape=jax.ShapeDtypeStruct((weights.shape[0], pieces[0].shape[1]), dtype),
        compiler_params=pltpu.CompilerParams(vmem_limit_bytes=VMEM_LIMIT),
        name="alpha_product",
    )(weights, *adds, *pieces)


def send(x, edges):
    return lax.ppermute(x, "alpha", [(s * CORES + c, t * CORES + c) for s, t in edges for c in range(CORES)])


def swap(x, chips):
    return lax.ppermute(x, "alpha", [(p * CORES + c, p * CORES + 1 - c) for p in chips for c in range(CORES)])


def gate(*values):
    return lax.optimization_barrier(values)


def block_ids(places, rows):
    ids = np.full((len(places), CORES, len(places[0])), -1, np.int32)
    for p, line in enumerate(places):
        for g, place in enumerate(line):
            if place is not None:
                for c in range(CORES):
                    ids[p, c, g] = (place[0] * CORES + c) * rows + place[1]
    return ids


def per_device(coefficients, diagonal, alpha_blocks, alpha_lists, beta_blocks, beta_lists):
    block = alpha_blocks.shape[2]
    rows_a, rows_b = alpha_blocks.shape[0], beta_blocks.shape[0]
    chips = lax.axis_size("alpha") // CORES
    owners_b = lax.axis_size("beta")
    index_a, index_b = lax.axis_index("alpha"), lax.axis_index("beta")

    pack, beta_ids = beta_tables(beta_lists, index_b, owners_b, rows_b)
    mine_b = lax.dynamic_slice_in_dim(beta_lists, index_b * rows_b, rows_b, 0)

    def place(chip, first, count):
        return [(chip, first + g) if 0 <= chip < chips else None for g in range(count)]

    mine_a = lax.dynamic_slice_in_dim(alpha_lists, index_a * rows_a, rows_a, 0)

    def table_of(places):
        ids = [block_ids(p, rows_a) for p in places]
        ids = jnp.asarray(np.concatenate(ids + [i[:, ::-1] for i in ids], axis=2).reshape(chips * CORES, -1))
        return slot_table(mine_a, lax.dynamic_index_in_dim(ids, index_a, 0, keepdims=False))

    table_b = slot_table(mine_b, beta_ids)

    def exchange():
        packed = pack_beta(pack, coefficients, owners_b, block)
        return lax.all_to_all(packed, "beta", split_axis=0, concat_axis=0, tiled=True)

    everyone = range(chips)
    own = [place(p, 0, rows_a) for p in everyone]
    if chips == 4:
        far, near = [(0, 2), (1, 3), (2, 0), (3, 1)], [(0, 1), (1, 0), (2, 3), (3, 2)]
        far_from, near_from, both_from = [2, 3, 0, 1], [1, 0, 3, 2], [3, 2, 1, 0]


        cuts = [(0, FIRST), (FIRST, rows_a - FIRST)]

        def of(chip_of, first=0, count=rows_a):
            return [place(chip_of[p], first, count) for p in everyone]

        table_here = table_of([own, of(near_from)] + [of(far_from, *cut) for cut in cuts] + [of(both_from, *cuts[0])])
        table_last = table_of([of(both_from, *cuts[1])])
        half = table_last.shape[1] // 2
        tables = (table_here, table_last[:, :half], table_last[:, half:])

        far_own = [send(coefficients[f * block : (f + n) * block], far) for f, n in cuts]
        near_own = send(coefficients, near)
        near_far = send(far_own[0], near)
        own_swapped = swap(coefficients, everyone)
        arrived = exchange()
        near_far, far_own[1], here, table_b, *tables = gate(near_far, far_own[1], coefficients, table_b, *tables)
        near_last = send(far_own[1], near)
        pieces = [here, near_own, *far_own, near_far]
        pieces += [own_swapped] + [swap(x, everyone) for x in pieces[1:]]
        *pieces, here, blocks_here, arrived = gate(*pieces, here, alpha_blocks, arrived)
        weights = [lay_out(table, blocks_here) for table in tables]
        acc = alpha_product(weights[0], pieces, None, jnp.float32)
        acc = beta_product(table_b, beta_blocks, here, diagonal, arrived, acc)
        near_last, acc, *weights = gate(near_last, acc, *weights)
        acc = alpha_product(weights[1], [near_last], acc, jnp.float32)
        return alpha_product(weights[2], [swap(near_last, everyone)], acc, jnp.bfloat16)

    arrived = exchange()
    pieces, places = [coefficients], [own]
    left, right = [], []
    for u in range((chips - 1) * rows_a):
        kind, v = u // rows_a, u % rows_a
        mine = coefficients[v * block : (v + 1) * block]
        left.append(send(mine if u < rows_a else left[u - rows_a], [(p, p - 1) for p in range(1, chips) if kind < chips - p]))
        right.append(send(mine if u < rows_a else right[u - rows_a], [(p, p + 1) for p in range(chips - 1) if kind < p + 1]))
        pieces += [left[u], right[u]]
        places += [[place(p + 1 + kind, v, 1) for p in everyone], [place(p - 1 - kind, v, 1) for p in everyone]]
    acc = jnp.zeros(diagonal.shape, jnp.float32)
    acc = beta_product(table_b, beta_blocks, coefficients, diagonal, arrived, acc)
    step = 2 * rows_a
    for k in range(0, len(pieces), step):
        last = k + step >= len(pieces)
        weights = lay_out(table_of(places[k : k + step]), alpha_blocks)
        xs = pieces[k : k + step] + [swap(x, everyone) for x in pieces[k : k + step]]
        acc = alpha_product(weights, xs, acc, jnp.bfloat16 if last else jnp.float32)
    return acc


def solution(mesh):
    in_specs = (
        P("alpha", "beta"),
        P("alpha", "beta"),
        P("alpha", None, None, None),
        P(),
        P("beta", None, None, None),
        P(),
    )
    out_specs = P("alpha", "beta")
    return jax.shard_map(
        per_device, mesh=mesh, in_specs=in_specs, out_specs=out_specs, check_vma=False
    )
```
